32 devices in a mesh: section: 2 (over x), fsdp: 4 (over z), tensor: 4 (over y, core).
Axes of the slice: x: 2, y: 2, z: 4, core: 2. Of those that a mesh axis runs over, the one named last changes fastest.
Arguments:
- tokens: bfloat16 [8192, 768], P('fsdp'), may hold values from -6 to 6
- segment_ids: int32 [8, 1024], P('fsdp'), may hold values from 0 to 5, never falling along the last dimension, each value on 1 to 512 neighbouring positions
- ln_gain: bfloat16 [2, 2, 768], P('section', None, 'fsdp'), may hold values from 0.5 to 1.5
- ln_bias: bfloat16 [2, 2, 768], P('section', None, 'fsdp'), may hold values from -1.75 to 1.75
- w_qkv: bfloat16 [2, 768, 3, 768], P('section', 'fsdp', None, 'tensor'), may hold values from -0.21875 to 0.21875
- b_qkv: bfloat16 [2, 3, 768], P('section', None, 'tensor'), may hold values from -3 to 3
- w_o: bfloat16 [2, 768, 768], P('section', 'tensor', 'fsdp'), may hold values from -0.875 to 0.875
- b_o: bfloat16 [2, 768], P('section', 'fsdp'), may hold values from -1.75 to 1.75
- w_in: bfloat16 [2, 768, 3072], P('section', 'fsdp', 'tensor'), may hold values from -0.21875 to 0.21875
- b_in: bfloat16 [2, 3072], P('section', 'tensor'), may hold values from -3 to 3
- w_out: bfloat16 [2, 3072, 768], P('section', 'tensor', 'fsdp'), may hold values from -0.109375 to 0.109375
- b_out: bfloat16 [2, 768], P('section', 'fsdp'), may hold values from -1.75 to 1.75
- cotangent: bfloat16 [8192, 768], P('fsdp'), may hold values from -6 to 6
Outputs:
- layer_out: bfloat16 [2, 8192, 768], P('section', 'fsdp')
- input_grad: bfloat16 [2, 8192, 768], P('section', 'fsdp')
- grad_ln_gain: float32 [2, 2, 768], P('section', None, 'fsdp')
- grad_ln_bias: float32 [2, 2, 768], P('section', None, 'fsdp')
- grad_w_qkv: float32 [2, 768, 3, 768], P('section', 'fsdp', None, 'tensor')
- grad_b_qkv: float32 [2, 3, 768], P('section', None, 'tensor')
- grad_w_o: float32 [2, 768, 768], P('section', 'tensor', 'fsdp')
- grad_b_o: float32 [2, 768], P('section', 'fsdp')
- grad_w_in: float32 [2, 768, 3072], P('section', 'fsdp', 'tensor')
- grad_b_in: float32 [2, 3072], P('section', 'tensor')
- grad_w_out: float32 [2, 3072, 768], P('section', 'tensor', 'fsdp')
- grad_b_out: float32 [2, 768], P('section', 'fsdp')
The draws below stay inside these ranges and needn't reach their ends.
Inputs may be any that keep to these rules, and one draw needn't show every extreme that they name: `segment_ids`: along each sequence the ids never fall; each of the 6 documents has 1 to 512 tokens, and one has exactly 512.
All inputs are finite; a program needn't handle non-finite values.
Results may differ from the reference program's by a relative error of at most 0.023.
Values may be sent and summed in bfloat16 or wider, within the bound.
A program may use at most 256 MiB of HBM per device.

```python
import math
import jax
import jax.numpy as jnp
import numpy as np
from jax import lax

D = 768
FF = 3072
HEAD = 64
LAYERS = 2
SEQ = 1024
DOCS = 6
SEQS = 8
TOKENS = 8192
N_TENSOR = 4


def steps_of(key, extent, pieces, least, top_value):
    level, own = 1.0, jax.random.fold_in(key, 6)
    for dim, parts in pieces:
        heights = jnp.exp(jax.random.uniform(jax.random.fold_in(own, dim), (parts,), jnp.float32, least / len(pieces), top_value / len(pieces)))
        level = level * jnp.repeat(heights, extent[dim] // parts).reshape([-1 if axis == dim else 1 for axis in range(len(extent))])
    return level


def profile(number_of, total, most, slope):
    loads = [(1 << 20) // math.isqrt(rank ** slope) + 1 for rank in range(2, number_of + 1)]
    surplus, holding = total - most - (number_of - 1), [1] * (number_of - 1)
    while surplus > 0:
        free = [i for i in range(number_of - 1) if holding[i] < most]
        whole, left = sum([loads[i] for i in free]), surplus
        for i in free:
            addition = min(most - holding[i], max(1, left * loads[i] // whole), surplus)
            holding[i] = holding[i] + addition
            surplus = surplus - addition
    return np.array([most] + holding)


def uneven(rng, number_of, total, most, skew):
    if number_of == 2:
        one = jax.random.randint(rng, (), max(1, total - most), min(most, total - 1) + 1)
        return jnp.stack([one, total - one])
    sizes = jnp.asarray(profile(number_of, total, most, skew), jnp.int32)
    couples = (number_of - 1) // 2
    donor, receiver = sizes[1:1 + 2 * couples:2], sizes[2:2 + 2 * couples:2]
    margin = jnp.minimum(donor - 1, most - receiver)
    shifted = jax.random.randint(jax.random.fold_in(rng, 1), (couples,), 0, 1 << 20) % (margin + 1)
    sizes = sizes.at[1:1 + 2 * couples:2].set(donor - shifted).at[2:2 + 2 * couples:2].set(receiver + shifted)
    return sizes[jax.random.permutation(jax.random.fold_in(rng, 2), number_of)]


def noise(stream_key, extent, scale, reach, split=(), kind=jnp.bfloat16):
    level = steps_of(stream_key, extent, split, -0.22, 0.18) if split else 1.0
    values = jax.random.normal(stream_key, extent, jnp.float32) * scale * level
    return jnp.minimum(jnp.maximum(values, -reach), reach).astype(kind)


def setup_inputs(seed: int = 0) -> dict:
    seeds = jax.random.split(jax.random.key(seed), 14)
    tokens = noise(seeds[0], (TOKENS, D), 1.0, 6.0, ((0, 4),))
    segment_ids = jax.vmap(lambda own: jnp.searchsorted(jnp.cumsum(uneven(own, DOCS, SEQ, SEQ // 2, 2)), jnp.arange(SEQ), side="right"))(jax.random.split(seeds[1], SEQS)).reshape((SEQS, SEQ)).astype(jnp.int32)
    ln_gain = jnp.clip(1.0 + 0.1 * jax.random.normal(seeds[2], (LAYERS, 2, D), jnp.float32), 0.5, 1.5).astype(jnp.bfloat16)
    ln_bias = noise(seeds[3], (LAYERS, 2, D), 0.3, 1.75, ((0, 2), (2, 4)))
    w_qkv = noise(seeds[4], (LAYERS, D, 3, D), D ** -0.5, 0.21875, ((0, 2), (1, 4), (3, 4)))
    b_qkv = noise(seeds[5], (LAYERS, 3, D), 0.5, 3.0, ((0, 2), (2, 4)))
    w_o = noise(seeds[6], (LAYERS, D, D), (D // 16) ** -0.5, 0.875, ((0, 2), (1, 4), (2, 4)))
    b_o = noise(seeds[7], (LAYERS, D), 0.3, 1.75, ((0, 2), (1, 4)))
    w_in = noise(seeds[8], (LAYERS, D, FF), D ** -0.5, 0.21875, ((0, 2), (1, 4), (2, 4)))
    b_in = noise(seeds[9], (LAYERS, FF), 0.5, 3.0, ((0, 2), (1, 4)))
    w_out = noise(seeds[10], (LAYERS, FF, D), FF ** -0.5, 0.109375, ((0, 2), (1, 4), (2, 4)))
    b_out = noise(seeds[11], (LAYERS, D), 0.3, 1.75, ((0, 2), (1, 4)))
    cotangent = noise(seeds[12], (TOKENS, D), 1.0, 6.0, ((0, 4),))
    return {"tokens": tokens, "segment_ids": segment_ids, "ln_gain": ln_gain, "ln_bias": ln_bias, "w_qkv": w_qkv, "b_qkv": b_qkv, "w_o": w_o, "b_o": b_o, "w_in": w_in, "b_in": b_in, "w_out": w_out, "b_out": b_out, "cotangent": cotangent}


@jax.custom_vjp
def low(v):
    return lax.optimization_barrier(v.astype(jnp.bfloat16)).astype(jnp.float32)

@jax.custom_vjp
def low_back(v):
    return v

def low_keep(v):
    return (low(v), None)

def low_pass(kept, grad):
    return (grad,)

def back_keep(v):
    return (v, None)

def back_low(kept, grad):
    return (low(grad),)
low.defvjp(low_keep, low_pass)
low_back.defvjp(back_keep, back_low)
eps_norm = 1e-05
highest = lax.Precision.HIGHEST

def norm_pair(row_data, gain_rows, shift_rows):
    row_mean = lax.optimization_barrier(jnp.mean(row_data, axis=-1, keepdims=True))
    centred = row_data - row_mean
    row_var = lax.optimization_barrier(jnp.mean(centred * centred, axis=-1, keepdims=True))
    scaled = centred * lax.rsqrt(row_var + eps_norm)
    return (scaled * gain_rows[0] + shift_rows[0], scaled * gain_rows[1] + shift_rows[1])

def positions_within(segment):
    positions = jnp.arange(segment.shape[0], dtype=jnp.int32)
    starts = jnp.concatenate([jnp.ones((1,), jnp.bool_), segment[1:] != segment[:-1]])
    first_row = lax.cummax(jnp.where(starts, positions, jnp.zeros_like(positions)), axis=0)
    return (positions - first_row).astype(jnp.float32)

def rotary_tables(segment, head_size):
    half_width = head_size // 8
    freq_table = 10000.0 ** (-2.0 * jnp.arange(half_width, dtype=jnp.float32) / (head_size // 4))
    angle_table = positions_within(segment)[:, None] * freq_table[None, :]
    cos_table = jnp.concatenate([jnp.cos(angle_table), jnp.cos(angle_table)], axis=-1)
    sine_table = jnp.concatenate([jnp.sin(angle_table), jnp.sin(angle_table)], axis=-1)
    return (cos_table, sine_table)

def rotate(vectors, cos_table, sine_table):
    rot_width = cos_table.shape[-1]
    part_rot = vectors[..., :rot_width]
    lower_half = part_rot[..., :rot_width // 2]
    upper_half = part_rot[..., rot_width // 2:]
    turned = jnp.concatenate([-upper_half, lower_half], axis=-1)
    rotated = part_rot * cos_table[:, None, :] + turned * sine_table[:, None, :]
    return jnp.concatenate([rotated, vectors[..., rot_width:]], axis=-1)

def attend_ref(query_heads, key_heads, values, segment):
    length = query_heads.shape[0]
    block_rows = min(512, length)
    block_count = length // block_rows
    positions = jnp.arange(length, dtype=jnp.int32)

    def block_fn(block_args):
        query_blk, seg_blk, row_blk = block_args
        scores = low_back(jnp.einsum('qhe,khe->hqk', query_blk, key_heads, precision=highest))
        allowed = (positions[None, :] <= row_blk[:, None]) & (seg_blk[:, None] == segment[None, :])
        scores = jnp.where(allowed[None], scores, -1000000000.0)
        softmax_w = low(jax.nn.softmax(scores, axis=-1))
        return jnp.einsum('hqk,khe->qhe', softmax_w, values, precision=highest)
    blocks = lax.map(jax.checkpoint(block_fn), (query_heads.reshape(block_count, block_rows, -1, HEAD), segment.reshape(block_count, block_rows), positions.reshape(block_count, block_rows)))
    return blocks.reshape(length, -1, HEAD)

def layer_sequence(row_data, segment, weights):
    gain_rows, shift_rows, w_qkv, b_qkv, w_o, b_o, w_in, b_in, w_out, b_out = weights
    h_one, h_two = norm_pair(row_data, gain_rows, shift_rows)
    h_one = low(h_one)
    h_two = low(h_two)
    cos_table, sine_table = rotary_tables(segment, HEAD)
    col_width = D // N_TENSOR
    unit_count = FF // N_TENSOR
    length = row_data.shape[0]
    summed = jnp.zeros_like(row_data)
    for group_index in range(N_TENSOR):
        col_range = slice(group_index * col_width, (group_index + 1) * col_width)
        unit_range = slice(group_index * unit_count, (group_index + 1) * unit_count)
        joined_qkv = low_back(jnp.einsum('rd,dsc->rsc', h_one, w_qkv[:, :, col_range], precision=highest) + b_qkv[None, :, col_range])
        query_heads = low(rotate(joined_qkv[:, 0].reshape(length, -1, HEAD), cos_table, sine_table) * (1.0 / math.sqrt(HEAD)))
        key_heads = low(rotate(joined_qkv[:, 1].reshape(length, -1, HEAD), cos_table, sine_table))
        values = low(joined_qkv[:, 2].reshape(length, -1, HEAD))
        head_mix = attend_ref(query_heads, key_heads, values, segment).reshape(length, col_width)
        head_mix = low(low_back(head_mix))
        pre_active = low_back(jnp.dot(h_two, w_in[:, unit_range], precision=highest) + b_in[unit_range])
        active = low(jax.nn.gelu(pre_active, approximate=False))
        branch = jnp.dot(head_mix, w_o[col_range], precision=highest) + jnp.dot(active, w_out[unit_range], precision=highest)
        summed = summed + low(branch)
    return row_data + summed + b_o + b_out

def run_layer(row_data, segments, weights):

    def scan_step(loop_carry, seq_item):
        return (loop_carry, layer_sequence(seq_item[0], seq_item[1], weights))
    return lax.scan(scan_step, jnp.zeros((), jnp.float32), (row_data, segments))[1]

def reference(tokens, segment_ids, ln_gain, ln_bias, w_qkv, b_qkv, w_o, b_o, w_in, b_in, w_out, b_out, cotangent):
    params = tuple((item.astype(jnp.float32) for item in (ln_gain, ln_bias, w_qkv, b_qkv, w_o, b_o, w_in, b_in, w_out, b_out)))
    start_rows = tokens.astype(jnp.float32).reshape(SEQS, SEQ, D)
    probe_zero = jnp.zeros_like(start_rows)

    def forward(start_rows, probe_zero, params):
        first_out = run_layer(start_rows, segment_ids, tuple((item[0] for item in params)))
        second_in = low_back(low(first_out)) + probe_zero
        second_out = run_layer(second_in, segment_ids, tuple((item[1] for item in params)))
        return (second_out, first_out)
    second_out, pull_back, first_out = jax.vjp(forward, start_rows, probe_zero, params, has_aux=True)
    d_start, d_probe, d_params = pull_back(cotangent.astype(jnp.float32).reshape(SEQS, SEQ, D))
    layer_out = jnp.stack([first_out, second_out]).reshape(LAYERS, TOKENS, D).astype(jnp.bfloat16)
    input_grad = jnp.stack([d_start, d_probe]).reshape(LAYERS, TOKENS, D).astype(jnp.bfloat16)
    return (layer_out, input_grad, d_params[0], d_params[1], d_params[2], d_params[3], d_params[4], d_params[5], d_params[6], d_params[7], d_params[8], d_params[9])
```

```python
import functools
import math

import jax
import jax.numpy as jnp
from jax import lax
from jax.experimental import pallas as pl
from jax.experimental.pallas import tpu as pltpu
from jax.sharding import PartitionSpec as P

HEAD = 64
PAD = 256
BLOCK = 256
REACH = 512
eps_norm = 1e-05
VMEM_LIMIT = 56 * 1024 * 1024
F32 = jnp.float32
BF16 = jnp.bfloat16


def dot(a, b):
    return jnp.dot(a, b, preferred_element_type=F32)


def dot_t(a, b):
    return lax.dot_general(a, b, (((1,), (1,)), ((), ())), preferred_element_type=F32)


def dot_s(a, b):
    return lax.dot_general(a, b, (((0,), (0,)), ((), ())), preferred_element_type=F32)


def turn(t):
    width = t.shape[-1]
    lane = lax.broadcasted_iota(jnp.int32, t.shape, 1) % HEAD
    return jnp.where(lane < HEAD // 8, -pltpu.roll(t, width - HEAD // 8, 1), pltpu.roll(t, HEAD // 8, 1))


def normed(rows):
    mean = jnp.mean(rows, axis=-1, keepdims=True)
    centred = rows - mean
    var = jnp.mean(centred * centred, axis=-1, keepdims=True)
    inv = lax.rsqrt(var + eps_norm)
    return centred * inv, inv


def tables(cos_ref, sin_ref, rows):
    cos, sin = cos_ref[rows, :], sin_ref[rows, :]
    return jnp.concatenate([cos, cos], axis=1), jnp.concatenate([sin, sin], axis=1)


def head_mask(shape, head):
    lane = lax.broadcasted_iota(jnp.int32, shape, 1)
    return (lane >= head * HEAD) & (lane < (head + 1) * HEAD)


def allowed_keys(segc_ref, segr_ref, low, start, stop):
    shape = (stop - start, stop - low)
    row = start + lax.broadcasted_iota(jnp.int32, shape, 0)
    col = low + lax.broadcasted_iota(jnp.int32, shape, 1)
    return (col <= row) & (segc_ref[start:stop, :] == segr_ref[:, low:stop])


def windows(length):
    return [(max(0, i - REACH), i, i + BLOCK) for i in range(0, length, BLOCK)]


def forward_kernel(
    heads, ff, x_ref, w_ref, vec_ref, bias_ref, cos_ref, sin_ref, segc_ref, segr_ref,
    part_ref, q_ref, k_ref, v_ref, o_ref, lse_ref, m_ref, slope_ref, h1_ref, h2_ref,
):
    length = x_ref.shape[0]
    base = 2 * ff

    @pl.loop(0, length // BLOCK)
    def _(step):
        rows = pl.ds(pl.multiple_of(step * BLOCK, BLOCK), BLOCK)
        xhat, _ = normed(x_ref[rows, :].astype(F32))
        h1 = (xhat * vec_ref[0:1, :] + vec_ref[2:3, :]).astype(BF16)
        h2 = (xhat * vec_ref[1:2, :] + vec_ref[3:4, :]).astype(BF16)
        h1_ref[rows, :] = h1
        h2_ref[rows, :] = h2
        cos, sin = tables(cos_ref, sin_ref, rows)
        q = dot(h1, w_ref[:, base : base + PAD]) + bias_ref[:, ff : ff + PAD]
        k = dot(h1, w_ref[:, base + PAD : base + 2 * PAD]) + bias_ref[:, ff + PAD : ff + 2 * PAD]
        v = dot(h1, w_ref[:, base + 2 * PAD : base + 3 * PAD]) + bias_ref[:, ff + 2 * PAD : ff + 3 * PAD]
        q_ref[rows, :] = ((q * cos + turn(q) * sin) * (1.0 / math.sqrt(HEAD))).astype(BF16)
        k_ref[rows, :] = (k * cos + turn(k) * sin).astype(BF16)
        v_ref[rows, :] = v.astype(BF16)
        a = dot(h2, w_ref[:, 0:ff]) + bias_ref[:, 0:ff]
        cdf = 0.5 * (1.0 + lax.erf(a * (1.0 / math.sqrt(2.0))))
        m = (a * cdf).astype(BF16)
        m_ref[rows, :] = m
        density = jnp.exp(-0.5 * a * a) * (1.0 / math.sqrt(2.0 * math.pi))
        slope_ref[rows, :] = (cdf + a * density).astype(BF16)

    for low, start, stop in windows(length):
        allowed = allowed_keys(segc_ref, segr_ref, low, start, stop)
        q = q_ref[start:stop, :]
        keys, values = k_ref[low:stop, :], v_ref[low:stop, :]
        mix = jnp.zeros((BLOCK, PAD), F32)
        lses = jnp.zeros((BLOCK, 128), F32)
        lane = lax.broadcasted_iota(jnp.int32, (BLOCK, 128), 1)
        for head in range(heads):
            mask = head_mask((BLOCK, PAD), head)
            s = dot_t(jnp.where(mask, q, jnp.zeros_like(q)), keys)
            s = jnp.where(allowed, s, -1000000000.0)
            top = jnp.max(s, axis=-1, keepdims=True)
            e = jnp.exp(s - top)
            total = jnp.sum(e, axis=-1, keepdims=True)
            p = (e * (1.0 / total)).astype(BF16)
            mix = jnp.where(mask, dot(p, values), mix)
            lses = jnp.where(lane == head, top + jnp.log(total), lses)
        o = mix.astype(BF16)
        o_ref[start:stop, :] = o
        lse_ref[start:stop, :] = lses
        part_ref[start:stop, :] = (
            dot_t(o, w_ref[:, base + 3 * PAD : base + 4 * PAD]) + dot_t(m_ref[start:stop, :], w_ref[:, ff : 2 * ff])
        ).astype(BF16)


def backward_kernel(
    heads, ff, x_ref, dy_ref, w_ref, vec_ref, cos_ref, sin_ref, segc_ref, segr_ref,
    q_ref, k_ref, v_ref, lse_ref, slope_ref,
    dx_ref, da_ref, dqkv_ref, sums_ref, bsum_ref,
    dh2_ref, do_ref, dq_ref, dk_ref, dv_ref,
):
    length, width = x_ref.shape
    base = 2 * ff
    sums_ref[...] = jnp.zeros_like(sums_ref)
    bsum_ref[...] = jnp.zeros_like(bsum_ref)
    dk_ref[...] = jnp.zeros_like(dk_ref)
    dv_ref[...] = jnp.zeros_like(dv_ref)

    @pl.loop(0, length // BLOCK)
    def _(step):
        rows = pl.ds(pl.multiple_of(step * BLOCK, BLOCK), BLOCK)
        dy = dy_ref[rows, :]
        do_ref[rows, :] = dot(dy, w_ref[:, base + 3 * PAD : base + 4 * PAD]).astype(BF16)
        da = (dot(dy, w_ref[:, ff : 2 * ff]) * slope_ref[rows, :].astype(F32)).astype(BF16)
        da_ref[rows, :] = da
        bsum_ref[0:1, 0:ff] += jnp.sum(da.astype(F32), axis=0, keepdims=True)
        dh2_ref[rows, :] = dot_t(da, w_ref[:, 0:ff])

    for low, start, stop in windows(length):
        allowed = allowed_keys(segc_ref, segr_ref, low, start, stop)
        q, do = q_ref[start:stop, :], do_ref[start:stop, :]
        keys, values = k_ref[low:stop, :], v_ref[low:stop, :]
        dq = jnp.zeros((BLOCK, PAD), F32)
        for head in range(heads):
            mask = head_mask((BLOCK, PAD), head)
            q_h = jnp.where(mask, q, jnp.zeros_like(q))
            do_h = jnp.where(mask, do, jnp.zeros_like(do))
            s = jnp.where(allowed, dot_t(q_h, keys), -1000000000.0)
            p = jnp.exp(s - lse_ref[start:stop, head : head + 1])
            dp = dot_t(do_h, values)
            ds = (p * (dp - jnp.sum(p * dp, axis=-1, keepdims=True))).astype(BF16)
            dq = jnp.where(mask, dot(ds, keys), dq)
            dk_ref[low:stop, :] += dot_s(ds, q_h)
            dv_ref[low:stop, :] += dot_s(p.astype(BF16), do_h)
        dq_ref[start:stop, :] = dq

    @pl.loop(0, length // BLOCK)
    def _(step):
        rows = pl.ds(pl.multiple_of(step * BLOCK, BLOCK), BLOCK)
        cos, sin = tables(cos_ref, sin_ref, rows)
        dq, dk = dq_ref[rows, :], dk_ref[rows, :]
        dq = (dq * cos - turn(dq) * sin) * (1.0 / math.sqrt(HEAD))
        dk = dk * cos - turn(dk) * sin
        dqkv = jnp.concatenate([dq, dk, dv_ref[rows, :]], axis=1).astype(BF16)
        dqkv_ref[rows, :] = dqkv
        bsum_ref[0:1, ff : ff + 3 * PAD] += jnp.sum(dqkv.astype(F32), axis=0, keepdims=True)
        dh1 = dot_t(dqkv, w_ref[:, base : base + 3 * PAD])
        dh2 = dh2_ref[rows, :]
        xhat, inv = normed(x_ref[rows, :].astype(F32))
        sums_ref[0:1, :] += jnp.sum(dh1 * xhat, axis=0, keepdims=True)
        sums_ref[1:2, :] += jnp.sum(dh2 * xhat, axis=0, keepdims=True)
        sums_ref[2:3, :] += jnp.sum(dh1, axis=0, keepdims=True)
        sums_ref[3:4, :] += jnp.sum(dh2, axis=0, keepdims=True)
        sums_ref[4:5, :] += jnp.sum(dy_ref[rows, :].astype(F32), axis=0, keepdims=True)
        e = dh1 * vec_ref[0:1, :] + dh2 * vec_ref[1:2, :]
        mean_e = jnp.mean(e, axis=-1, keepdims=True)
        mean_ex = jnp.mean(e * xhat, axis=-1, keepdims=True)
        dx_ref[rows, :] = ((e - mean_e - xhat * mean_ex) * inv).astype(BF16)


def weight_kernel(ff, h1_ref, h2_ref, da_ref, dqkv_ref, dy_ref, m_ref, o_ref, g_ref):
    def fill(left_ref, right_ref, offset):
        @pl.loop(0, right_ref.shape[1] // 256)
        def _(step):
            at = pl.multiple_of(step * 256, 256)
            g_ref[:, pl.ds(offset + at, 256)] = dot_s(left_ref[...], right_ref[:, pl.ds(at, 256)]).astype(BF16)

    fill(h2_ref, da_ref, 0)
    fill(dy_ref, m_ref, ff)
    fill(h1_ref, dqkv_ref, 2 * ff)
    fill(dy_ref, o_ref, 2 * ff + 3 * PAD)


def call(kernel, outs, scratch=(), flops=0):
    vm = pl.BlockSpec(memory_space=pltpu.VMEM)

    def run(*args):
        return pl.pallas_call(
            kernel,
            out_shape=[jax.ShapeDtypeStruct(*o) for o in outs],
            in_specs=[vm] * len(args),
            out_specs=[vm] * len(outs),
            scratch_shapes=list(scratch),
            compiler_params=pltpu.CompilerParams(vmem_limit_bytes=VMEM_LIMIT),
            cost_estimate=pl.CostEstimate(flops=flops, bytes_accessed=20_000_000, transcendentals=0),
        )(*args)

    return run


def positions_within(segment):
    positions = jnp.arange(segment.shape[0], dtype=jnp.int32)
    starts = jnp.concatenate([jnp.ones((1,), jnp.bool_), segment[1:] != segment[:-1]])
    first_row = lax.cummax(jnp.where(starts, positions, jnp.zeros_like(positions)), axis=0)
    return (positions - first_row).astype(F32)


def rotary_tables(segment):
    half = HEAD // 8
    freq = 10000.0 ** (-2.0 * jnp.arange(half, dtype=F32) / (HEAD // 4))
    angle = positions_within(segment)[:, None] * freq[None, :]
    cos, sin = jnp.cos(angle), jnp.sin(angle)
    length = segment.shape[0]
    rest = HEAD - 2 * half
    one, zero = jnp.ones((length, rest), F32), jnp.zeros((length, rest), F32)
    return (
        jnp.concatenate([cos, cos, one] * 2, axis=1),
        jnp.concatenate([sin, sin, zero] * 2, axis=1),
    )


def widen(t):
    return jnp.pad(t, [(0, 0)] * (t.ndim - 1) + [(0, PAD - t.shape[-1])])


def per_device(
    tokens, segment_ids, ln_gain, ln_bias, w_qkv, b_qkv, w_o, b_o, w_in, b_in, w_out, b_out, cotangent,
):
    seq_len = segment_ids.shape[1]
    width = tokens.shape[1]
    ff = w_in.shape[2]
    cols = w_o.shape[1]
    heads = cols // HEAD
    piece = w_in.shape[1]
    section = lax.axis_index("section")
    sections = lax.axis_size("section")
    both = ("section", "fsdp")

    small = jnp.concatenate([ln_gain[0], ln_bias[0], b_o, b_out], axis=0).T
    qkv = widen(w_qkv[0]).reshape(piece, 3 * PAD)
    last = jnp.concatenate([w_o[0].T, small, jnp.zeros((piece, PAD - cols - 6), BF16)], axis=1)
    packed = jnp.concatenate([w_in[0], w_out[0].T, qkv, last], axis=1)
    weights = lax.all_gather(packed, both, axis=0, tiled=True).reshape(sections, width, -1)
    biases = jnp.concatenate([b_in, widen(b_qkv[0]).reshape(1, 3 * PAD)], axis=1).astype(F32)
    biases = lax.all_gather(biases, "section", axis=0, tiled=True)
    at = 2 * ff + 3 * PAD + cols
    vectors = jnp.pad(jnp.swapaxes(weights[:, :, at : at + 6], 1, 2).astype(F32), ((0, 0), (0, 2), (0, 0)))

    rows0 = lax.dynamic_slice_in_dim(tokens, section * seq_len, seq_len, 0)
    upstream = lax.dynamic_slice_in_dim(cotangent, section * seq_len, seq_len, 0)
    segment = lax.dynamic_index_in_dim(segment_ids, section, 0, keepdims=False)
    cos, sin = rotary_tables(segment)
    segc, segr = segment[:, None], segment[None, :]

    forward = call(
        functools.partial(forward_kernel, heads, ff),
        [
            ((seq_len, width), BF16), ((seq_len, PAD), BF16), ((seq_len, PAD), BF16), ((seq_len, PAD), BF16),
            ((seq_len, PAD), BF16), ((seq_len, 128), F32), ((seq_len, ff), BF16), ((seq_len, ff), BF16),
            ((seq_len, width), BF16), ((seq_len, width), BF16),
        ],
        flops=5_000_000_000,
    )
    backward = call(
        functools.partial(backward_kernel, heads, ff),
        [
            ((seq_len, width), BF16), ((seq_len, ff), BF16), ((seq_len, 3 * PAD), BF16), ((8, width), F32),
            ((8, ff + 3 * PAD), F32),
        ],
        [
            pltpu.VMEM((seq_len, width), F32), pltpu.VMEM((seq_len, PAD), BF16), pltpu.VMEM((seq_len, PAD), F32),
            pltpu.VMEM((seq_len, PAD), F32), pltpu.VMEM((seq_len, PAD), F32),
        ],
        flops=8_000_000_000,
    )
    weight_grads = call(
        functools.partial(weight_kernel, ff), [((width, 2 * ff + 4 * PAD), BF16)], flops=4_000_000_000
    )

    def run_forward(rows, layer):
        out = forward(rows, weights[layer], vectors[layer], biases[layer][None], cos, sin, segc, segr)
        summed = lax.psum(out[0], "tensor").astype(F32)
        vec = vectors[layer]
        return (rows.astype(F32) + summed + vec[4] + vec[5]).astype(BF16), out[1:]

    def run_backward(rows, dy, layer, saved):
        q, k, v, o, lse, m, slope, h1, h2 = saved
        dx, da, dqkv, sums, bsum = backward(
            rows, dy, weights[layer], vectors[layer], cos, sin, segc, segr, q, k, v, lse, slope
        )
        dx = lax.psum(dx, "tensor").astype(F32)
        (grads,) = weight_grads(h1, h2, da, dqkv, dy, m, o)
        return (dy.astype(F32) + dx).astype(BF16), grads, sums, bsum

    out0, saved0 = run_forward(rows0, 0)
    out1, saved1 = run_forward(out0, 1)
    grad1, gw1, sums1, bsum1 = run_backward(out0, upstream, 1, saved1)
    part1 = lax.psum_scatter(gw1, "fsdp", scatter_dimension=0, tiled=True)
    grad0, gw0, sums0, bsum0 = run_backward(rows0, grad1, 0, saved0)
    part0 = lax.psum_scatter(gw0, "fsdp", scatter_dimension=0, tiled=True)

    down, up = [(1, 0)], [(0, 1)]
    at_first = section == 0

    def exchange(first, second):
        from_one = lax.ppermute(first, "section", down)
        from_zero = lax.ppermute(second, "section", up)
        return jnp.where(at_first, first, second), jnp.where(at_first, from_one, from_zero)

    def whole(first, second):
        own, other = exchange(first, second)
        return jnp.concatenate([jnp.where(at_first, own, other), jnp.where(at_first, other, own)], axis=0)

    outputs = whole(out0, out1)
    input_grads = whole(grad0, grad1)
    own, other = exchange(part0, part1)
    grads = own.astype(F32) + other.astype(F32)

    scale = 1.0 / lax.axis_size("tensor")
    sums = jnp.stack([sums0, sums1])
    sums = jnp.concatenate([sums[:, :4], sums[:, 4:5] * scale], axis=1)
    sums = lax.psum(sums, ("section", "fsdp", "tensor"))
    sums = lax.dynamic_index_in_dim(sums, section, 0, keepdims=False)
    sums = lax.dynamic_slice_in_dim(sums, lax.axis_index("fsdp") * piece, piece, 1)
    bsum = lax.psum(jnp.stack([bsum0[0], bsum1[0]]), both)
    bsum = lax.dynamic_index_in_dim(bsum, section, 0, keepdims=False)
    g_qkv = grads[:, 2 * ff : 2 * ff + 3 * PAD].reshape(piece, 3, PAD)[:, :, :cols]
    return (
        outputs[None],
        input_grads[None],
        sums[0:2][None],
        sums[2:4][None],
        g_qkv[None],
        bsum[ff:].reshape(3, PAD)[:, :cols][None],
        grads[:, 2 * ff + 3 * PAD : 2 * ff + 3 * PAD + cols].T[None],
        sums[4][None],
        grads[:, 0:ff][None],
        bsum[0:ff][None],
        grads[:, ff : 2 * ff].T[None],
        sums[4][None],
    )


def solution(mesh):
    in_specs = (
        P("fsdp", None),
        P("fsdp", None),
        P("section", None, "fsdp"),
        P("section", None, "fsdp"),
        P("section", "fsdp", None, "tensor"),
        P("section", None, "tensor"),
        P("section", "tensor", "fsdp"),
        P("section", "fsdp"),
        P("section", "fsdp", "tensor"),
        P("section", "tensor"),
        P("section", "tensor", "fsdp"),
        P("section", "fsdp"),
        P("fsdp", None),
    )
    out_specs = (
        P("section", "fsdp", None),
        P("section", "fsdp", None),
        P("section", None, "fsdp"),
        P("section", None, "fsdp"),
        P("section", "fsdp", None, "tensor"),
        P("section", None, "tensor"),
        P("section", "tensor", "fsdp"),
        P("section", "fsdp"),
        P("section", "fsdp", "tensor"),
        P("section", "tensor"),
        P("section", "tensor", "fsdp"),
        P("section", "fsdp"),
    )
    return jax.shard_map(
        per_device, mesh=mesh, in_specs=in_specs, out_specs=out_specs, check_vma=False
    )
```

```python
import functools
import math

import jax
import jax.numpy as jnp
from jax import lax
from jax.experimental import pallas as pl
from jax.experimental.pallas import tpu as pltpu
from jax.sharding import PartitionSpec as P

HEAD = 64
PAD = 256
BLOCK = 256
REACH = 512
eps_norm = 1e-05
VMEM_LIMIT = 56 * 1024 * 1024
F32 = jnp.float32
BF16 = jnp.bfloat16


def dot(a, b):
    return jnp.dot(a, b, preferred_element_type=F32)


def dot_t(a, b):
    return lax.dot_general(a, b, (((1,), (1,)), ((), ())), preferred_element_type=F32)


def dot_s(a, b):
    return lax.dot_general(a, b, (((0,), (0,)), ((), ())), preferred_element_type=F32)


def turn(t):
    width = t.shape[-1]
    lane = lax.broadcasted_iota(jnp.int32, t.shape, 1) % HEAD
    return jnp.where(lane < HEAD // 8, -pltpu.roll(t, width - HEAD // 8, 1), pltpu.roll(t, HEAD // 8, 1))


def normed(rows):
    mean = jnp.mean(rows, axis=-1, keepdims=True)
    centred = rows - mean
    var = jnp.mean(centred * centred, axis=-1, keepdims=True)
    inv = lax.rsqrt(var + eps_norm)
    return centred * inv, inv


def tables(cos_ref, sin_ref, rows):
    cos, sin = cos_ref[rows, :], sin_ref[rows, :]
    return jnp.concatenate([cos, cos], axis=1), jnp.concatenate([sin, sin], axis=1)


def head_mask(shape, head):
    lane = lax.broadcasted_iota(jnp.int32, shape, 1)
    return (lane >= head * HEAD) & (lane < (head + 1) * HEAD)


def allowed_keys(segc_ref, segr_ref, low, start, stop):
    shape = (stop - start, stop - low)
    row = start + lax.broadcasted_iota(jnp.int32, shape, 0)
    col = low + lax.broadcasted_iota(jnp.int32, shape, 1)
    return (col <= row) & (segc_ref[start:stop, :] == segr_ref[:, low:stop])


def windows(length):
    return [(max(0, i - REACH), i, i + BLOCK) for i in range(0, length, BLOCK)]


def forward_kernel(
    heads, ff, x_ref, w_ref, vec_ref, bias_ref, cos_ref, sin_ref, segc_ref, segr_ref,
    part_ref, q_ref, k_ref, v_ref, o_ref, lse_ref, m_ref, slope_ref, h1_ref, h2_ref,
):
    length = x_ref.shape[0]
    base = 2 * ff

    @pl.loop(0, length // BLOCK)
    def _(step):
        rows = pl.ds(pl.multiple_of(step * BLOCK, BLOCK), BLOCK)
        xhat, _ = normed(x_ref[rows, :].astype(F32))
        h1 = (xhat * vec_ref[0:1, :] + vec_ref[2:3, :]).astype(BF16)
        h2 = (xhat * vec_ref[1:2, :] + vec_ref[3:4, :]).astype(BF16)
        h1_ref[rows, :] = h1
        h2_ref[rows, :] = h2
        cos, sin = tables(cos_ref, sin_ref, rows)
        q = dot(h1, w_ref[:, base : base + PAD]) + bias_ref[:, ff : ff + PAD]
        k = dot(h1, w_ref[:, base + PAD : base + 2 * PAD]) + bias_ref[:, ff + PAD : ff + 2 * PAD]
        v = dot(h1, w_ref[:, base + 2 * PAD : base + 3 * PAD]) + bias_ref[:, ff + 2 * PAD : ff + 3 * PAD]
        q_ref[rows, :] = ((q * cos + turn(q) * sin) * (1.0 / math.sqrt(HEAD))).astype(BF16)
        k_ref[rows, :] = (k * cos + turn(k) * sin).astype(BF16)
        v_ref[rows, :] = v.astype(BF16)
        a = dot(h2, w_ref[:, 0:ff]) + bias_ref[:, 0:ff]
        cdf = 0.5 * (1.0 + lax.erf(a * (1.0 / math.sqrt(2.0))))
        m = (a * cdf).astype(BF16)
        m_ref[rows, :] = m
        density = jnp.exp(-0.5 * a * a) * (1.0 / math.sqrt(2.0 * math.pi))
        slope_ref[rows, :] = (cdf + a * density).astype(BF16)

    for low, start, stop in windows(length):
        allowed = allowed_keys(segc_ref, segr_ref, low, start, stop)
        q = q_ref[start:stop, :]
        keys, values = k_ref[low:stop, :], v_ref[low:stop, :]
        mix = jnp.zeros((BLOCK, PAD), F32)
        lses = jnp.zeros((BLOCK, 128), F32)
        lane = lax.broadcasted_iota(jnp.int32, (BLOCK, 128), 1)
        for head in range(heads):
            mask = head_mask((BLOCK, PAD), head)
            s = dot_t(jnp.where(mask, q, jnp.zeros_like(q)), keys)
            s = jnp.where(allowed, s, -1000000000.0)
            top = jnp.max(s, axis=-1, keepdims=True)
            e = jnp.exp(s - top)
            total = jnp.sum(e, axis=-1, keepdims=True)
            p = (e * (1.0 / total)).astype(BF16)
            mix = jnp.where(mask, dot(p, values), mix)
            lses = jnp.where(lane == head, top + jnp.log(total), lses)
        o = mix.astype(BF16)
        o_ref[start:stop, :] = o
        lse_ref[start:stop, :] = lses
        part_ref[start:stop, :] = (
            dot_t(o, w_ref[:, base + 3 * PAD : base + 4 * PAD]) + dot_t(m_ref[start:stop, :], w_ref[:, ff : 2 * ff])
        ).astype(BF16)


def backward_kernel(
    heads, ff, x_ref, dy_ref, w_ref, vec_ref, cos_ref, sin_ref, segc_ref, segr_ref,
    q_ref, k_ref, v_ref, lse_ref, slope_ref,
    dx_ref, da_ref, dqkv_ref, sums_ref, bsum_ref,
    dh2_ref, do_ref, dq_ref, dk_ref, dv_ref,
):
    length, width = x_ref.shape
    base = 2 * ff
    sums_ref[...] = jnp.zeros_like(sums_ref)
    bsum_ref[...] = jnp.zeros_like(bsum_ref)
    dk_ref[...] = jnp.zeros_like(dk_ref)
    dv_ref[...] = jnp.zeros_like(dv_ref)

    @pl.loop(0, length // BLOCK)
    def _(step):
        rows = pl.ds(pl.multiple_of(step * BLOCK, BLOCK), BLOCK)
        dy = dy_ref[rows, :]
        do_ref[rows, :] = dot(dy, w_ref[:, base + 3 * PAD : base + 4 * PAD]).astype(BF16)
        da = (dot(dy, w_ref[:, ff : 2 * ff]) * slope_ref[rows, :].astype(F32)).astype(BF16)
        da_ref[rows, :] = da
        bsum_ref[0:1, 0:ff] += jnp.sum(da.astype(F32), axis=0, keepdims=True)
        dh2_ref[rows, :] = dot_t(da, w_ref[:, 0:ff])

    for low, start, stop in windows(length):
        allowed = allowed_keys(segc_ref, segr_ref, low, start, stop)
        q, do = q_ref[start:stop, :], do_ref[start:stop, :]
        keys, values = k_ref[low:stop, :], v_ref[low:stop, :]
        dq = jnp.zeros((BLOCK, PAD), F32)
        for head in range(heads):
            mask = head_mask((BLOCK, PAD), head)
            q_h = jnp.where(mask, q, jnp.zeros_like(q))
            do_h = jnp.where(mask, do, jnp.zeros_like(do))
            s = jnp.where(allowed, dot_t(q_h, keys), -1000000000.0)
            p = jnp.exp(s - lse_ref[start:stop, head : head + 1])
            dp = dot_t(do_h, values)
            ds = (p * (dp - jnp.sum(p * dp, axis=-1, keepdims=True))).astype(BF16)
            dq = jnp.where(mask, dot(ds, keys), dq)
            dk_ref[low:stop, :] += dot_s(ds, q_h)
            dv_ref[low:stop, :] += dot_s(p.astype(BF16), do_h)
        dq_ref[start:stop, :] = dq

    @pl.loop(0, length // BLOCK)
    def _(step):
        rows = pl.ds(pl.multiple_of(step * BLOCK, BLOCK), BLOCK)
        cos, sin = tables(cos_ref, sin_ref, rows)
        dq, dk = dq_ref[rows, :], dk_ref[rows, :]
        dq = (dq * cos - turn(dq) * sin) * (1.0 / math.sqrt(HEAD))
        dk = dk * cos - turn(dk) * sin
        dqkv = jnp.concatenate([dq, dk, dv_ref[rows, :]], axis=1).astype(BF16)
        dqkv_ref[rows, :] = dqkv
        bsum_ref[0:1, ff : ff + 3 * PAD] += jnp.sum(dqkv.astype(F32), axis=0, keepdims=True)
        dh1 = dot_t(dqkv, w_ref[:, base : base + 3 * PAD])
        dh2 = dh2_ref[rows, :]
        xhat, inv = normed(x_ref[rows, :].astype(F32))
        sums_ref[0:1, :] += jnp.sum(dh1 * xhat, axis=0, keepdims=True)
        sums_ref[1:2, :] += jnp.sum(dh2 * xhat, axis=0, keepdims=True)
        sums_ref[2:3, :] += jnp.sum(dh1, axis=0, keepdims=True)
        sums_ref[3:4, :] += jnp.sum(dh2, axis=0, keepdims=True)
        sums_ref[4:5, :] += jnp.sum(dy_ref[rows, :].astype(F32), axis=0, keepdims=True)
        e = dh1 * vec_ref[0:1, :] + dh2 * vec_ref[1:2, :]
        mean_e = jnp.mean(e, axis=-1, keepdims=True)
        mean_ex = jnp.mean(e * xhat, axis=-1, keepdims=True)
        dx_ref[rows, :] = ((e - mean_e - xhat * mean_ex) * inv).astype(BF16)


def weight_kernel(ff, h1_ref, h2_ref, da_ref, dqkv_ref, dy_ref, m_ref, o_ref, g_ref):
    def fill(left_ref, right_ref, offset):
        @pl.loop(0, right_ref.shape[1] // 256)
        def _(step):
            at = pl.multiple_of(step * 256, 256)
            g_ref[:, pl.ds(offset + at, 256)] = dot_s(left_ref[...], right_ref[:, pl.ds(at, 256)]).astype(BF16)

    fill(h2_ref, da_ref, 0)
    fill(dy_ref, m_ref, ff)
    fill(h1_ref, dqkv_ref, 2 * ff)
    fill(dy_ref, o_ref, 2 * ff + 3 * PAD)


def call(kernel, outs, scratch=(), flops=0):
    vm = pl.BlockSpec(memory_space=pltpu.VMEM)

    def run(*args):
        return pl.pallas_call(
            kernel,
            out_shape=[jax.ShapeDtypeStruct(*o) for o in outs],
            in_specs=[vm] * len(args),
            out_specs=[vm] * len(outs),
            scratch_shapes=list(scratch),
            compiler_params=pltpu.CompilerParams(vmem_limit_bytes=VMEM_LIMIT),
            cost_estimate=pl.CostEstimate(flops=flops, bytes_accessed=20_000_000, transcendentals=0),
        )(*args)

    return run


def positions_within(segment):
    positions = jnp.arange(segment.shape[0], dtype=jnp.int32)
    starts = jnp.concatenate([jnp.ones((1,), jnp.bool_), segment[1:] != segment[:-1]])
    first_row = lax.cummax(jnp.where(starts, positions, jnp.zeros_like(positions)), axis=0)
    return (positions - first_row).astype(F32)


def rotary_tables(segment):
    half = HEAD // 8
    freq = 10000.0 ** (-2.0 * jnp.arange(half, dtype=F32) / (HEAD // 4))
    angle = positions_within(segment)[:, None] * freq[None, :]
    cos, sin = jnp.cos(angle), jnp.sin(angle)
    length = segment.shape[0]
    rest = HEAD - 2 * half
    one, zero = jnp.ones((length, rest), F32), jnp.zeros((length, rest), F32)
    return (
        jnp.concatenate([cos, cos, one] * 2, axis=1),
        jnp.concatenate([sin, sin, zero] * 2, axis=1),
    )


def tensor_sum(part):
    devices = range(lax.axis_size("tensor"))
    index = lax.axis_index("tensor")

    def halves(block, bit):
        size = block.shape[0] // 2
        place = (index // bit) % 2
        keep = lax.dynamic_slice_in_dim(block, place * size, size, 0)
        send = lax.dynamic_slice_in_dim(block, (1 - place) * size, size, 0)
        got = lax.ppermute(send, "tensor", [(i, i ^ bit) for i in devices])
        return (keep.astype(F32) + got.astype(F32)).astype(BF16)

    def join(block, bit):
        first = (index // bit) % 2 == 0
        got = lax.ppermute(block, "tensor", [(i, i ^ bit) for i in devices])
        return jnp.concatenate([jnp.where(first, block, got), jnp.where(first, got, block)], axis=0)

    return join(join(halves(halves(part, 1), 2), 2), 1)


def widen(t):
    return jnp.pad(t, [(0, 0)] * (t.ndim - 1) + [(0, PAD - t.shape[-1])])


def per_device(
    tokens, segment_ids, ln_gain, ln_bias, w_qkv, b_qkv, w_o, b_o, w_in, b_in, w_out, b_out, cotangent,
):
    seq_len = segment_ids.shape[1]
    width = tokens.shape[1]
    ff = w_in.shape[2]
    cols = w_o.shape[1]
    heads = cols // HEAD
    piece = w_in.shape[1]
    section = lax.axis_index("section")
    sections = lax.axis_size("section")
    both = ("section", "fsdp")

    small = jnp.concatenate([ln_gain[0], ln_bias[0], b_o, b_out], axis=0).T
    qkv = widen(w_qkv[0]).reshape(piece, 3 * PAD)
    last = jnp.concatenate([w_o[0].T, small, jnp.zeros((piece, PAD - cols - 6), BF16)], axis=1)
    packed = jnp.concatenate([w_in[0], w_out[0].T, qkv, last], axis=1)
    weights = lax.all_gather(packed, both, axis=0, tiled=True).reshape(sections, width, -1)
    biases = jnp.concatenate([b_in, widen(b_qkv[0]).reshape(1, 3 * PAD)], axis=1).astype(F32)
    biases = lax.all_gather(biases, "section", axis=0, tiled=True)
    at = 2 * ff + 3 * PAD + cols
    vectors = jnp.pad(jnp.swapaxes(weights[:, :, at : at + 6], 1, 2).astype(F32), ((0, 0), (0, 2), (0, 0)))

    rows0 = lax.dynamic_slice_in_dim(tokens, section * seq_len, seq_len, 0)
    upstream = lax.dynamic_slice_in_dim(cotangent, section * seq_len, seq_len, 0)
    segment = lax.dynamic_index_in_dim(segment_ids, section, 0, keepdims=False)
    cos, sin = rotary_tables(segment)
    segc, segr = segment[:, None], segment[None, :]

    forward = call(
        functools.partial(forward_kernel, heads, ff),
        [
            ((seq_len, width), BF16), ((seq_len, PAD), BF16), ((seq_len, PAD), BF16), ((seq_len, PAD), BF16),
            ((seq_len, PAD), BF16), ((seq_len, 128), F32), ((seq_len, ff), BF16), ((seq_len, ff), BF16),
            ((seq_len, width), BF16), ((seq_len, width), BF16),
        ],
        flops=5_000_000_000,
    )
    backward = call(
        functools.partial(backward_kernel, heads, ff),
        [
            ((seq_len, width), BF16), ((seq_len, ff), BF16), ((seq_len, 3 * PAD), BF16), ((8, width), F32),
            ((8, ff + 3 * PAD), F32),
        ],
        [
            pltpu.VMEM((seq_len, width), F32), pltpu.VMEM((seq_len, PAD), BF16), pltpu.VMEM((seq_len, PAD), F32),
            pltpu.VMEM((seq_len, PAD), F32), pltpu.VMEM((seq_len, PAD), F32),
        ],
        flops=8_000_000_000,
    )
    weight_grads = call(
        functools.partial(weight_kernel, ff), [((width, 2 * ff + 4 * PAD), BF16)], flops=4_000_000_000
    )

    def run_forward(rows, layer):
        out = forward(rows, weights[layer], vectors[layer], biases[layer][None], cos, sin, segc, segr)
        summed = (lax.psum(out[0], "tensor") if layer == 0 else tensor_sum(out[0])).astype(F32)
        vec = vectors[layer]
        return (rows.astype(F32) + summed + vec[4] + vec[5]).astype(BF16), out[1:]

    def run_backward(rows, dy, layer, saved):
        q, k, v, o, lse, m, slope, h1, h2 = saved
        dx, da, dqkv, sums, bsum = backward(
            rows, dy, weights[layer], vectors[layer], cos, sin, segc, segr, q, k, v, lse, slope
        )
        dx = tensor_sum(dx)
        (grads,) = weight_grads(h1, h2, da, dqkv, dy, m, o)
        dx, grads = lax.optimization_barrier((dx, grads))
        dx = dx.astype(F32)
        return (dy.astype(F32) + dx).astype(BF16), grads, sums, bsum

    out0, saved0 = run_forward(rows0, 0)
    out1, saved1 = run_forward(out0, 1)
    grad1, gw1, sums1, bsum1 = run_backward(out0, upstream, 1, saved1)
    part1 = lax.psum_scatter(gw1, "fsdp", scatter_dimension=0, tiled=True)
    grad0, gw0, sums0, bsum0 = run_backward(rows0, grad1, 0, saved0)
    part0 = lax.psum_scatter(gw0, "fsdp", scatter_dimension=0, tiled=True)

    down, up = [(1, 0)], [(0, 1)]
    at_first = section == 0

    def exchange(first, second):
        from_one = lax.ppermute(first, "section", down)
        from_zero = lax.ppermute(second, "section", up)
        return jnp.where(at_first, first, second), jnp.where(at_first, from_one, from_zero)

    def whole(first, second):
        own, other = exchange(first, second)
        return jnp.concatenate([jnp.where(at_first, own, other), jnp.where(at_first, other, own)], axis=0)

    outputs = whole(out0, out1)
    input_grads = whole(grad0, grad1)
    own, other = exchange(part0, part1)
    grads = own.astype(F32) + other.astype(F32)

    scale = 1.0 / lax.axis_size("tensor")
    sums = jnp.stack([sums0, sums1])
    sums = jnp.concatenate([sums[:, :4], sums[:, 4:5] * scale], axis=1)
    sums = lax.psum(sums, ("section", "fsdp", "tensor"))
    sums = lax.dynamic_index_in_dim(sums, section, 0, keepdims=False)
    sums = lax.dynamic_slice_in_dim(sums, lax.axis_index("fsdp") * piece, piece, 1)
    bsum = lax.psum(jnp.stack([bsum0[0], bsum1[0]]), both)
    bsum = lax.dynamic_index_in_dim(bsum, section, 0, keepdims=False)
    g_qkv = grads[:, 2 * ff : 2 * ff + 3 * PAD].reshape(piece, 3, PAD)[:, :, :cols]
    return (
        outputs[None],
        input_grads[None],
        sums[0:2][None],
        sums[2:4][None],
        g_qkv[None],
        bsum[ff:].reshape(3, PAD)[:, :cols][None],
        grads[:, 2 * ff + 3 * PAD : 2 * ff + 3 * PAD + cols].T[None],
        sums[4][None],
        grads[:, 0:ff][None],
        bsum[0:ff][None],
        grads[:, ff : 2 * ff].T[None],
        sums[4][None],
    )


def solution(mesh):
    in_specs = (
        P("fsdp", None),
        P("fsdp", None),
        P("section", None, "fsdp"),
        P("section", None, "fsdp"),
        P("section", "fsdp", None, "tensor"),
        P("section", None, "tensor"),
        P("section", "tensor", "fsdp"),
        P("section", "fsdp"),
        P("section", "fsdp", "tensor"),
        P("section", "tensor"),
        P("section", "tensor", "fsdp"),
        P("section", "fsdp"),
        P("fsdp", None),
    )
    out_specs = (
        P("section", "fsdp", None),
        P("section", "fsdp", None),
        P("section", None, "fsdp"),
        P("section", None, "fsdp"),
        P("section", "fsdp", None, "tensor"),
        P("section", None, "tensor"),
        P("section", "tensor", "fsdp"),
        P("section", "fsdp"),
        P("section", "fsdp", "tensor"),
        P("section", "tensor"),
        P("section", "tensor", "fsdp"),
        P("section", "fsdp"),
    )
    return jax.shard_map(
        per_device, mesh=mesh, in_specs=in_specs, out_specs=out_specs, check_vma=False
    )
```
